256 devices in a mesh: row: 16 (over y, x_lo, core), col: 16 (over z, x_hi).
Axes of the slice: x: 4 (x_hi: 2, x_lo: 2; x = x_hi * 2 + x_lo), y: 4, z: 8, core: 2. Of those that a mesh axis runs over, the one named last changes fastest.
Arguments:
- weight_tiles: bfloat16 [4096, 8192], P('row', 'col'), may hold values from -6 to 6
- expand_rows: bfloat16 [5120, 4096], P(None, 'row'), may hold values from -0.125 to 0.125
- expand_cols: bfloat16 [10240, 8192], P('row', 'col'), may hold values from -0.09375 to 0.09375
Outputs:
- grown: bfloat16 [5120, 10240], P('row', 'col')
The draws below stay inside these ranges and needn't reach their ends.
All inputs are finite; a program needn't handle non-finite values.
Results may differ from the reference program's by a relative error of at most 0.0049.
Values may be sent and summed in bfloat16 or wider, within the bound.
No kernel may reach another device: no remote copies, remote signals or barrier semaphores. Data moves between devices by JAX's collectives and lax.ppermute only.
A program may use at most 128 MiB of HBM per device.

```python
import jax
import jax.numpy as jnp
from jax import lax

D = 8192
DN = 10240
HOLD = 4096
HNEW = 5120
N_COL = 16


def strengthened(values, key, source, target, shards_of, factor):
    def block_of(axis_at):
        return (jnp.arange(values.shape[axis_at]) // (values.shape[axis_at] // shards_of)).reshape((-1,) + (1,) * (values.ndim - 1 - axis_at))

    near = jax.random.permutation(key, shards_of)[block_of(target)]
    far = (block_of(target) + shards_of // 2) % shards_of
    return jnp.where((block_of(source) == near) | (block_of(source) == far), factor * values, values)


def steps_of(rng, dims, split, smallest, top_value):
    level = 1.0
    for dim, parts in split:
        heights = jax.random.uniform(jax.random.fold_in(jax.random.fold_in(rng, 6), dim), (parts,), jnp.float32, smallest / len(split), top_value / len(split))
        level = level * jnp.repeat(jnp.exp(heights), dims[dim] // parts).reshape((-1,) + (1,) * (len(dims) - 1 - dim))
    return level


def gaussian(rng, extent, scale, bound, pieces=(), kind=jnp.bfloat16):
    array = jax.random.normal(rng, extent, jnp.float32) * scale
    if len(pieces) > 0:
        array = steps_of(rng, extent, pieces, -0.22, 0.18) * array
    return jnp.clip(array, min=-bound, max=bound).astype(kind)


def heavy_noise(key, shape, deviation, bound, split, heavy, held_as=jnp.bfloat16):
    drawn = deviation * jax.random.normal(key, shape, jnp.float32)
    if split:
        drawn = drawn * steps_of(key, shape, split, -0.22, 0.18)
    return jnp.clip(strengthened(drawn, jax.random.fold_in(key, 3), *heavy), -bound, bound).astype(held_as)


def setup_inputs(seed: int = 0) -> dict:
    splits = jax.random.split(jax.random.key(seed), 4)
    weight_tiles = gaussian(splits[0], (HOLD, D), 1.0, 6.0, ((0, 16), (1, 16)))
    expand_rows = heavy_noise(splits[1], (HNEW, HOLD), HOLD ** -0.5, 0.125, ((1, 16),), (1, 0, 16, 2.0))
    expand_cols = heavy_noise(splits[2], (DN, D), D ** -0.5, 0.09375, ((0, 16), (1, 16)), (1, 0, 16, 2.0))
    return dict(weight_tiles=weight_tiles, expand_rows=expand_rows, expand_cols=expand_cols)


def reference(weight_tiles, expand_rows, expand_cols):
    block_width = D // N_COL

    def add_block(total, index):
        start = index * block_width
        left = lax.dynamic_slice_in_dim(weight_tiles, start, block_width, 1)
        right = lax.dynamic_slice_in_dim(expand_cols, start, block_width, 1)
        part = lax.dot_general(left, right, (((1,), (1,)), ((), ())), preferred_element_type=jnp.float32)
        return total + part, None

    start_total = jnp.zeros((HOLD, DN), jnp.float32)
    indices = jnp.arange(N_COL, dtype=jnp.int32)
    total, unused = lax.scan(add_block, start_total, indices)
    stretched = total.astype(jnp.bfloat16)
    return jnp.dot(expand_rows, stretched, preferred_element_type=jnp.float32).astype(jnp.bfloat16)
```

```python
import jax
import jax.numpy as jnp
from jax import lax
from jax.sharding import Mesh, PartitionSpec as P

AXES = ("y", "xl", "core", "z", "xh")
SIZES = (4, 2, 2, 8, 2)


def pairs(move):
    ids = {}
    for i in range(256):
        rest, at = i, []
        for size in reversed(SIZES):
            at.append(rest % size)
            rest //= size
        ids[tuple(reversed(at))] = i
    return [(i, ids[move(*at)]) for at, i in ids.items()]


def send(value, move):
    return lax.ppermute(value, AXES, pairs(move))


def other_core(y, xl, co, z, xh):
    return y, xl, 1 - co, z, xh


def y_up(y, xl, co, z, xh):
    return (y + 1) % 4, xl, co, z, xh


def y_down(y, xl, co, z, xh):
    return (y - 1) % 4, xl, co, z, xh


def z_up(y, xl, co, z, xh):
    return y, xl, co, (z + 1) % 8, xh


def z_down(y, xl, co, z, xh):
    return y, xl, co, (z - 1) % 8, xh


def in_run(y, xl, co, z, xh):
    return y, 1 - xl, co, z, xh


def out_run(y, xl, co, z, xh):
    return y, 1 - xl, co, z, 1 - xh


def dispatch(j):
    def move(y, xl, co, z, xh):
        p = (z + j) % 8
        return p // 2, p % 2, co, 2 * y + xl, xh

    return move


def rotated(stack, start):
    n = stack.shape[0]
    return lax.dynamic_slice_in_dim(jnp.concatenate([stack, stack]), start, n, 0)


def dot_f32(left, right):
    return lax.dot_general(
        left, right, (((0, 2), (0, 2)), ((), ())), preferred_element_type=jnp.float32
    )


def on_device(weight_tiles, expand_rows, expand_cols):
    y, xl, co, z, xh = (lax.axis_index(a) for a in AXES)
    p = 2 * y + xl
    bf16 = jnp.bfloat16
    k1, width = weight_tiles.shape
    half = width // 2
    m = expand_rows.shape[0] // 16
    n = expand_cols.shape[0]
    quarter = n // 4

    rows = expand_rows.reshape(4, 2, 2, m, k1)
    mine = lax.dynamic_index_in_dim(rows, co, 2, keepdims=False)
    theirs = lax.dynamic_index_in_dim(rows, 1 - co, 2, keepdims=False)
    got_rows = send(theirs, other_core)
    got_tiles = send(weight_tiles, other_core)

    pieces = expand_cols.reshape(4, quarter, 2, half).transpose(0, 2, 1, 3)
    pieces = rotated(pieces.reshape(8, quarter, half), z)
    got = [send(pieces[j], dispatch(j)) for j in range(8)]

    left = jnp.concatenate([mine, got_rows], -1).reshape(8 * m, 2 * k1)
    right = jnp.concatenate([weight_tiles, got_tiles], 0)
    part = [
        jnp.dot(left, right[:, i * half : (i + 1) * half], preferred_element_type=jnp.float32)
        .astype(bf16).reshape(4, 2 * m, half)
        for i in range(2)
    ]
    part = jnp.stack(part, 1).reshape(8, 2 * m, half)
    part = lax.all_to_all(part, ("y", "xl"), 0, 0, tiled=True)
    inner = jnp.sum(part.astype(jnp.float32), 0).astype(bf16)
    inner = jnp.where(xl == 0, inner, jnp.concatenate([inner[m:], inner[:m]]))

    cols = rotated(jnp.stack(got[::-1]), (7 - p + z) % 8)
    below = send(cols, y_up)
    above = send(cols, y_down)
    far = jnp.concatenate([send(below[:4], y_up), send(above[4:], y_down)])
    full = jnp.zeros((8, n, half), bf16)
    for shift, block in ((0, cols), (1, above), (2, far), (3, below)):
        full = lax.dynamic_update_slice_in_dim(full, block, (y + shift) % 4 * quarter, 1)
    other = send(full, other_core)
    near_cols = jnp.where(xh == co, full, other)
    far_cols = jnp.where(xh == co, other, full)

    slots = [inner] + [None] * 7
    for i in range(1, 4):
        slots[i] = send(slots[i - 1], z_down)
        slots[-i] = send(slots[(-i + 1) % 8], z_up)
    slots[4] = jnp.concatenate([send(slots[3][:m], z_down), send(slots[5][m:], z_up)])
    inner_all = jnp.stack(slots)

    cross = dot_f32(inner_all, far_cols)
    cut = m // 2
    via_in = send(cross[:cut].astype(bf16), in_run)
    via_out = send(cross[cut:m].astype(bf16), out_run)
    straight = dot_f32(inner_all, near_cols)
    to_out = cross[m:] + jnp.pad(via_in.astype(jnp.float32), ((0, m - cut), (0, 0)))
    to_in = straight[m:] + jnp.pad(via_out.astype(jnp.float32), ((cut, 0), (0, 0)))
    from_out = send(to_out.astype(bf16), out_run)
    from_in = send(to_in.astype(bf16), in_run)
    total = straight[:m] + from_out.astype(jnp.float32) + from_in.astype(jnp.float32)
    return total.astype(bf16)


def solution(mesh):
    fine = Mesh(mesh.devices.reshape(SIZES), AXES)
    row, col = ("y", "xl", "core"), ("z", "xh")
    return jax.shard_map(
        on_device,
        mesh=fine,
        in_specs=(P(row, col), P(None, row), P(row, col)),
        out_specs=P(row, col),
        check_vma=False,
    )
```

```python
import jax
import jax.numpy as jnp
from jax import lax
from jax.sharding import Mesh, PartitionSpec as P

AXES = ("y", "xl", "core", "z", "xh")
SIZES = (4, 2, 2, 8, 2)


def pairs(move):
    ids = {}
    for i in range(256):
        rest, at = i, []
        for size in reversed(SIZES):
            at.append(rest % size)
            rest //= size
        ids[tuple(reversed(at))] = i
    return [(i, ids[move(*at)]) for at, i in ids.items()]


def send(value, move):
    return lax.ppermute(value, AXES, pairs(move))


def other_core(y, xl, co, z, xh):
    return y, xl, 1 - co, z, xh


def z_by(step):
    return lambda y, xl, co, z, xh: (y, xl, co, (z + step) % 8, xh)


def y_by(step):
    return lambda y, xl, co, z, xh: ((y + step) % 4, xl, co, z, xh)


def in_run(y, xl, co, z, xh):
    return y, 1 - xl, co, z, xh


def out_run(y, xl, co, z, xh):
    return y, 1 - xl, co, z, 1 - xh


def rotated(stack, start):
    n = stack.shape[0]
    return lax.dynamic_slice_in_dim(jnp.concatenate([stack, stack]), start, n, 0)


def dot_f32(left, right):
    return lax.dot_general(
        left, right, (((1,), (1,)), ((), ())), preferred_element_type=jnp.float32
    )


def on_device(weight_tiles, expand_rows, expand_cols):
    y, xl, co, z, xh = (lax.axis_index(a) for a in AXES)
    bf16 = jnp.bfloat16
    k1, width = weight_tiles.shape
    half = width // 2
    m = expand_rows.shape[0] // 16
    n = expand_cols.shape[0]
    quarter = n // 4

    rows = expand_rows.reshape(4, 2, 2, m, k1)
    mine = lax.dynamic_index_in_dim(rows, co, 2, keepdims=False)
    theirs = lax.dynamic_index_in_dim(rows, 1 - co, 2, keepdims=False)
    got_rows = send(theirs, other_core)
    got_tiles = send(weight_tiles, other_core)

    pieces = expand_cols.reshape(4, quarter, 2, half).transpose(0, 2, 1, 3)
    pieces = pieces.reshape(8, quarter, half)
    got_rows, got_tiles, pieces = lax.optimization_barrier((got_rows, got_tiles, pieces))
    pieces = lax.all_to_all(pieces, ("y", "xl"), 0, 0, tiled=True)

    left = jnp.concatenate([mine, got_rows], -1).reshape(8 * m, 2 * k1)
    right = jnp.concatenate([weight_tiles, got_tiles], 0)
    part = [
        jnp.dot(left, right[:, i * half : (i + 1) * half], preferred_element_type=jnp.float32)
        .astype(bf16).reshape(4, 2 * m, half)
        for i in range(2)
    ]
    part = jnp.stack(part, 1).reshape(8, 2 * m, half)
    pieces = rotated(pieces, z)
    part, pieces = lax.optimization_barrier((part, pieces))
    part = lax.all_to_all(part, ("y", "xl"), 0, 0, tiled=True)
    got = [pieces[0]] + [send(pieces[-i % 8], z_by(-i)) for i in range(1, 8)]
    inner = jnp.sum(part.astype(jnp.float32), 0).astype(bf16)
    inner = jnp.where(xl == 0, inner, jnp.concatenate([inner[m:], inner[:m]]))

    cols = jnp.concatenate(got, 1)
    below = send(cols, y_by(1))
    above = send(cols, y_by(-1))
    far = jnp.concatenate([send(below[:, : 4 * half], y_by(1)), send(above[:, 4 * half :], y_by(-1))], 1)
    full = jnp.zeros((n, 8 * half), bf16)
    for shift, block in ((0, cols), (1, above), (2, far), (3, below)):
        full = lax.dynamic_update_slice_in_dim(full, block, (y + shift) % 4 * quarter, 0)
    slots = [inner] + [None] * 7
    up = down = inner
    for i in range(1, 4):
        up, down = send(up, z_by(-1)), send(down, z_by(1))
        if i < 3:
            up, down = lax.optimization_barrier((up, down))
        else:
            up, down, full = lax.optimization_barrier((up, down, full))
        slots[i], slots[-i] = up, down
    other = send(full, other_core)
    slots[4] = jnp.concatenate([send(up[:m], z_by(-1)), send(down[m:], z_by(1))])
    inner_all = jnp.concatenate(slots, 1)
    near_cols = jnp.where(xh == co, full, other)
    far_cols = jnp.where(xh == co, other, full)

    cross = dot_f32(inner_all, far_cols)
    cut = m // 2
    via_in = send(cross[:cut].astype(bf16), in_run)
    via_out = send(cross[cut:m].astype(bf16), out_run)
    straight = dot_f32(inner_all, near_cols)
    to_out = cross[m:] + jnp.pad(via_in.astype(jnp.float32), ((0, m - cut), (0, 0)))
    to_in = straight[m:] + jnp.pad(via_out.astype(jnp.float32), ((cut, 0), (0, 0)))
    from_out = send(to_out.astype(bf16), out_run)
    from_in = send(to_in.astype(bf16), in_run)
    total = straight[:m] + from_out.astype(jnp.float32) + from_in.astype(jnp.float32)
    return total.astype(bf16)


def solution(mesh):
    fine = Mesh(mesh.devices.reshape(SIZES), AXES)
    row, col = ("y", "xl", "core"), ("z", "xh")
    return jax.shard_map(
        on_device,
        mesh=fine,
        in_specs=(P(row, col), P(None, row), P(row, col)),
        out_specs=P(row, col),
        check_vma=False,
    )
```

```python
import jax
import jax.numpy as jnp
from jax import lax
from jax.sharding import Mesh, PartitionSpec as P

AXES = ("y", "xl", "core", "z", "xh")
SIZES = (4, 2, 2, 8, 2)
ORDER = (0, 1, 7, 2, 6, 3, 5, 4)


def pairs(move):
    ids = {}
    for i in range(256):
        rest, at = i, []
        for size in reversed(SIZES):
            at.append(rest % size)
            rest //= size
        ids[tuple(reversed(at))] = i
    return [(i, ids[move(*at)]) for at, i in ids.items()]


def send(value, move):
    return lax.ppermute(value, AXES, pairs(move))


def other_core(y, xl, co, z, xh):
    return y, xl, 1 - co, z, xh


def z_by(step):
    return lambda y, xl, co, z, xh: (y, xl, co, (z + step) % 8, xh)


def y_by(step):
    return lambda y, xl, co, z, xh: ((y + step) % 4, xl, co, z, xh)


def rotated(stack, start):
    n = stack.shape[0]
    return lax.dynamic_slice_in_dim(jnp.concatenate([stack, stack]), start, n, 0)


def row_by(step, other):
    return lambda y, xl, co, z, xh: ((y + step) % 4, xl ^ other, co, z, xh)


def in_run(y, xl, co, z, xh):
    return y, 1 - xl, co, z, xh


def out_run(y, xl, co, z, xh):
    return y, 1 - xl, co, z, 1 - xh


def dot_f32(left, right):
    return lax.dot_general(
        left, right, (((1,), (1,)), ((), ())), preferred_element_type=jnp.float32
    )


def on_device(weight_tiles, expand_rows, expand_cols):
    y, xl, co, z, xh = (lax.axis_index(a) for a in AXES)
    bf16 = jnp.bfloat16
    k1, width = weight_tiles.shape
    half = width // 2
    m = expand_rows.shape[0] // 16
    n = expand_cols.shape[0]
    quarter = n // 4

    rows = expand_rows.reshape(4, 2, 2, m, k1)
    mine = lax.dynamic_index_in_dim(rows, co, 2, keepdims=False)
    theirs = lax.dynamic_index_in_dim(rows, 1 - co, 2, keepdims=False)
    got_rows = send(theirs, other_core)
    got_tiles = send(weight_tiles, other_core)

    pieces = [expand_cols[:, i * half : (i + 1) * half].reshape(4, 1, quarter, half) for i in range(2)]
    pieces = jnp.concatenate(pieces, 1).reshape(8, quarter, half)
    got_rows, got_tiles, pieces = lax.optimization_barrier((got_rows, got_tiles, pieces))
    pieces = lax.all_to_all(pieces, ("y", "xl"), 0, 0, tiled=True)

    left = jnp.concatenate([mine, got_rows], -1).reshape(8 * m, 2 * k1)
    right = jnp.concatenate([weight_tiles, got_tiles], 0)
    part = [
        jnp.dot(left, right[:, i * half : (i + 1) * half], preferred_element_type=jnp.float32)
        .astype(bf16).reshape(4, 2, m, half)
        for i in range(2)
    ]
    part = jnp.stack([part[0], part[1][:, ::-1]], 1).reshape(8, 2 * m, half)
    pieces = rotated(pieces, z)
    part, pieces = lax.optimization_barrier((part, pieces))
    barrier = lax.optimization_barrier
    part = lax.all_to_all(part, ("y", "xl"), 0, 0, tiled=True)

    got = {0: pieces[0]}
    for group in ((1, 7, 2, 6), (3, 5, 4)):
        got.update({i: send(pieces[-i % 8], z_by(-i)) for i in group})
        got, pieces = barrier((got, pieces))
    cols = jnp.concatenate([got[i] for i in ORDER], 1)
    part, cols = barrier((part, cols))
    inner = jnp.sum(part.astype(jnp.float32), 0).astype(bf16)

    up1, down1 = send(inner, z_by(-1)), send(inner, z_by(1))
    below, above = send(cols, y_by(1)), send(cols, y_by(-1))
    up1, down1 = barrier((up1, down1))
    up2, down2 = send(up1, z_by(-1)), send(down1, z_by(1))
    first = jnp.concatenate((inner, up1, down1), 1)
    up2, down2, below, above, first = barrier((up2, down2, below, above, first))
    up3, down3 = send(up2, z_by(-1)), send(down2, z_by(1))
    far = [send(below[:, : 4 * half], y_by(1)), send(above[:, 4 * half :], y_by(-1))]
    second = jnp.concatenate((up2, down2), 1)
    up3, down3, far, second = barrier((up3, down3, far, second))
    full = jnp.zeros((n, 8 * half), bf16)
    for shift, block in ((0, cols), (1, above), (3, below), (2, jnp.concatenate(far, 1))):
        full = lax.dynamic_update_slice_in_dim(full, block, (y + shift) % 4 * quarter, 0)
    other = send(full, other_core)
    across = jnp.concatenate([send(up3[:m], z_by(-1)), send(down3[m:], z_by(1))])
    third = jnp.concatenate((up3, down3, across), 1)
    near = jnp.where(xh == co, full, other)
    far = jnp.where(xh == co, other, full)

    def product(side):
        return (
            dot_f32(first, side[:, : 3 * half])
            + dot_f32(second, side[:, 3 * half : 5 * half])
            + dot_f32(third, side[:, 5 * half :])
        )

    cross = product(far)
    cut = m // 2
    via_in = send(cross[:cut].astype(bf16), in_run)
    via_out = send(cross[cut:m].astype(bf16), out_run)
    straight = product(near)
    to_out = cross[m:] + jnp.pad(via_in.astype(jnp.float32), ((0, m - cut), (0, 0)))
    to_in = straight[m:] + jnp.pad(via_out.astype(jnp.float32), ((cut, 0), (0, 0)))
    from_out = send(to_out.astype(bf16), out_run)
    from_in = send(to_in.astype(bf16), in_run)
    total = straight[:m] + from_out.astype(jnp.float32) + from_in.astype(jnp.float32)
    return total.astype(bf16)


def solution(mesh):
    fine = Mesh(mesh.devices.reshape(SIZES), AXES)
    row, col = ("y", "xl", "core"), ("z", "xh")
    return jax.shard_map(
        on_device,
        mesh=fine,
        in_specs=(P(row, col), P(None, row), P(row, col)),
        out_specs=P(row, col),
        check_vma=False,
    )
```

```python
import jax
import jax.numpy as jnp
from jax import lax
from jax.sharding import Mesh, PartitionSpec as P

AXES = ("y", "xl", "core", "z", "xh")
SIZES = (4, 2, 2, 8, 2)
ORDER = (0, 1, 7, 2, 6, 3, 5, 4)


def pairs(move):
    ids = {}
    for i in range(256):
        rest, at = i, []
        for size in reversed(SIZES):
            at.append(rest % size)
            rest //= size
        ids[tuple(reversed(at))] = i
    return [(i, ids[move(*at)]) for at, i in ids.items()]


def send(value, move):
    return lax.ppermute(value, AXES, pairs(move))


def other_core(y, xl, co, z, xh):
    return y, xl, 1 - co, z, xh


def z_by(step):
    return lambda y, xl, co, z, xh: (y, xl, co, (z + step) % 8, xh)


def y_by(step):
    return lambda y, xl, co, z, xh: ((y + step) % 4, xl, co, z, xh)


def rotated(stack, start):
    n = stack.shape[0]
    return lax.dynamic_slice_in_dim(jnp.concatenate([stack, stack]), start, n, 0)


def row_by(step, other):
    return lambda y, xl, co, z, xh: ((y + step) % 4, xl ^ other, co, z, xh)


def in_run(y, xl, co, z, xh):
    return y, 1 - xl, co, z, xh


def out_run(y, xl, co, z, xh):
    return y, 1 - xl, co, z, 1 - xh


def dot_f32(left, right):
    return lax.dot_general(
        left, right, (((1,), (1,)), ((), ())), preferred_element_type=jnp.float32
    )


def on_device(weight_tiles, expand_rows, expand_cols):
    y, xl, co, z, xh = (lax.axis_index(a) for a in AXES)
    bf16 = jnp.bfloat16
    k1, width = weight_tiles.shape
    half = width // 2
    m = expand_rows.shape[0] // 16
    n = expand_cols.shape[0]
    quarter = n // 4

    rows = expand_rows.reshape(4, 2, 2, m, k1)
    mine = lax.dynamic_index_in_dim(rows, co, 2, keepdims=False)
    theirs = lax.dynamic_index_in_dim(rows, 1 - co, 2, keepdims=False)
    got_rows = send(theirs, other_core)
    got_tiles = send(weight_tiles, other_core)

    pieces = [expand_cols[:, i * half : (i + 1) * half].reshape(4, 1, quarter, half) for i in range(2)]
    pieces = jnp.concatenate(pieces, 1).reshape(8, quarter, half)
    got_rows, got_tiles, pieces = lax.optimization_barrier((got_rows, got_tiles, pieces))
    pieces = lax.all_to_all(pieces, ("y", "xl"), 0, 0, tiled=True)

    left = jnp.concatenate([mine, got_rows], -1).reshape(8 * m, 2 * k1)
    right = jnp.concatenate([weight_tiles, got_tiles], 0)
    part = [
        jnp.dot(left, right[:, i * half : (i + 1) * half], preferred_element_type=jnp.float32)
        .astype(bf16).reshape(4, 2, m, half)
        for i in range(2)
    ]
    part = jnp.stack([part[0], part[1][:, ::-1]], 1).reshape(8, 2 * m, half)
    pieces = rotated(pieces, z)
    part, pieces = lax.optimization_barrier((part, pieces))
    barrier = lax.optimization_barrier
    part = lax.all_to_all(part, ("y", "xl"), 0, 0, tiled=True)

    got = {0: pieces[0]}
    for group in ((4, 3, 5, 1), (7, 2, 6)):
        got.update({i: send(pieces[-i % 8], z_by(-i)) for i in group})
        got, pieces = barrier((got, pieces))
    cols = jnp.concatenate([got[i] for i in ORDER], 1)
    part, cols = barrier((part, cols))
    inner = jnp.sum(part.astype(jnp.float32), 0).astype(bf16)

    up1, down1 = send(inner, z_by(-1)), send(inner, z_by(1))
    below, above = send(cols, y_by(1)), send(cols, y_by(-1))
    up1, down1 = barrier((up1, down1))
    up2, down2 = send(up1, z_by(-1)), send(down1, z_by(1))
    first = jnp.concatenate((inner, up1, down1), 1)
    up2, down2, below, above, first = barrier((up2, down2, below, above, first))
    up3, down3 = send(up2, z_by(-1)), send(down2, z_by(1))
    far = [send(below[:, : 4 * half], y_by(1)), send(above[:, 4 * half :], y_by(-1))]
    second = jnp.concatenate((up2, down2), 1)
    up3, down3, far, second = barrier((up3, down3, far, second))
    full = jnp.zeros((n, 8 * half), bf16)
    for shift, block in ((0, cols), (1, above), (3, below), (2, jnp.concatenate(far, 1))):
        full = lax.dynamic_update_slice_in_dim(full, block, (y + shift) % 4 * quarter, 0)
    other = send(full, other_core)
    across = jnp.concatenate([send(up3[:m], z_by(-1)), send(down3[m:], z_by(1))])
    third = jnp.concatenate((up3, down3, across), 1)
    near = jnp.where(xh == co, full, other)
    far = jnp.where(xh == co, other, full)

    def product(side):
        return (
            dot_f32(first, side[:, : 3 * half])
            + dot_f32(second, side[:, 3 * half : 5 * half])
            + dot_f32(third, side[:, 5 * half :])
        )

    cross = product(far)
    cut = m // 2
    via_in = send(cross[:cut].astype(bf16), in_run)
    via_out = send(cross[cut:m].astype(bf16), out_run)
    straight = product(near)
    to_out = cross[m:] + jnp.pad(via_in.astype(jnp.float32), ((0, m - cut), (0, 0)))
    to_in = straight[m:] + jnp.pad(via_out.astype(jnp.float32), ((cut, 0), (0, 0)))
    from_out = send(to_out.astype(bf16), out_run)
    from_in = send(to_in.astype(bf16), in_run)
    total = straight[:m] + from_out.astype(jnp.float32) + from_in.astype(jnp.float32)
    return total.astype(bf16)


def solution(mesh):
    fine = Mesh(mesh.devices.reshape(SIZES), AXES)
    row, col = ("y", "xl", "core"), ("z", "xh")
    return jax.shard_map(
        on_device,
        mesh=fine,
        in_specs=(P(row, col), P(None, row), P(row, col)),
        out_specs=P(row, col),
        check_vma=False,
    )
```

```python
import jax
import jax.numpy as jnp
from jax import lax
from jax.sharding import Mesh, PartitionSpec as P

AXES = ("y", "xl", "core", "z", "xh")
SIZES = (4, 2, 2, 8, 2)
ORDER = (0, 1, 7, 2, 6, 3, 5, 4)


def pairs(move):
    ids = {}
    for i in range(256):
        rest, at = i, []
        for size in reversed(SIZES):
            at.append(rest % size)
            rest //= size
        ids[tuple(reversed(at))] = i
    return [(i, ids[move(*at)]) for at, i in ids.items()]


def send(value, move):
    return lax.ppermute(value, AXES, pairs(move))


def other_core(y, xl, co, z, xh):
    return y, xl, 1 - co, z, xh


def z_by(step):
    return lambda y, xl, co, z, xh: (y, xl, co, (z + step) % 8, xh)


def y_by(step):
    return lambda y, xl, co, z, xh: ((y + step) % 4, xl, co, z, xh)


def rotated(stack, start):
    n = stack.shape[0]
    return lax.dynamic_slice_in_dim(jnp.concatenate([stack, stack]), start, n, 0)


def row_by(step, other):
    return lambda y, xl, co, z, xh: ((y + step) % 4, xl ^ other, co, z, xh)


def in_run(y, xl, co, z, xh):
    return y, 1 - xl, co, z, xh


def out_run(y, xl, co, z, xh):
    return y, 1 - xl, co, z, 1 - xh


def dot_f32(left, right):
    return lax.dot_general(
        left, right, (((1,), (1,)), ((), ())), preferred_element_type=jnp.float32
    )


def on_device(weight_tiles, expand_rows, expand_cols):
    y, xl, co, z, xh = (lax.axis_index(a) for a in AXES)
    bf16 = jnp.bfloat16
    k1, width = weight_tiles.shape
    half = width // 2
    m = expand_rows.shape[0] // 16
    n = expand_cols.shape[0]
    quarter = n // 4

    rows = expand_rows.reshape(4, 2, 2, m, k1)
    mine = lax.dynamic_index_in_dim(rows, co, 2, keepdims=False)
    theirs = lax.dynamic_index_in_dim(rows, 1 - co, 2, keepdims=False)
    got_rows = send(theirs, other_core)
    got_tiles = send(weight_tiles, other_core)

    pieces = [expand_cols[:, i * half : (i + 1) * half].reshape(4, 1, quarter, half) for i in range(2)]
    pieces = jnp.concatenate(pieces, 1).reshape(8, quarter, half)
    got_rows, got_tiles, pieces = lax.optimization_barrier((got_rows, got_tiles, pieces))
    pieces = lax.all_to_all(pieces, ("y", "xl"), 0, 0, tiled=True)

    left = jnp.concatenate([mine, got_rows], -1).reshape(8 * m, 2 * k1)
    right = jnp.concatenate([weight_tiles, got_tiles], 0)
    part = [
        jnp.dot(left, right[:, i * half : (i + 1) * half], preferred_element_type=jnp.float32)
        .astype(bf16).reshape(4, 2, m, half)
        for i in range(2)
    ]
    part = jnp.stack([part[0], part[1][:, ::-1]], 1).reshape(8, 2 * m, half)
    pieces = rotated(pieces, z)
    part, pieces = lax.optimization_barrier((part, pieces))
    barrier = lax.optimization_barrier
    part = lax.all_to_all(part, ("y", "xl"), 0, 0, tiled=True)

    got = {0: pieces[0]}
    for group in ((4, 3, 5, 1), (7, 2, 6)):
        got.update({i: send(pieces[-i % 8], z_by(-i)) for i in group})
        got, pieces = barrier((got, pieces))
    cols = jnp.concatenate([got[i] for i in ORDER], 1)
    part, cols = barrier((part, cols))
    inner = jnp.sum(part.astype(jnp.float32), 0).astype(bf16)

    up1, down1 = send(inner, z_by(-1)), send(inner, z_by(1))
    below, above = send(cols, y_by(1)), send(cols, y_by(-1))
    up1, down1 = barrier((up1, down1))
    up2, down2 = send(up1, z_by(-1)), send(down1, z_by(1))
    first = jnp.concatenate((inner, up1, down1), 1)
    up2, down2, below, above, first = barrier((up2, down2, below, above, first))
    up3, down3 = send(up2, z_by(-1)), send(down2, z_by(1))
    far = [send(below[:, : 4 * half], y_by(1)), send(above[:, 4 * half :], y_by(-1))]
    second = jnp.concatenate((up2, down2), 1)
    up3, down3, far, second = barrier((up3, down3, far, second))
    full = jnp.zeros((n, 8 * half), bf16)
    for shift, block in ((0, cols), (1, above), (3, below), (2, jnp.concatenate(far, 1))):
        full = lax.dynamic_update_slice_in_dim(full, block, (y + shift) % 4 * quarter, 0)
    other = send(full, other_core)
    across = send(up3, z_by(-1))
    third = jnp.concatenate((up3, down3, across), 1)
    near = jnp.where(xh == co, full, other)
    far = jnp.where(xh == co, other, full)

    def product(side):
        return (
            dot_f32(first, side[:, : 3 * half])
            + dot_f32(second, side[:, 3 * half : 5 * half])
            + dot_f32(third, side[:, 5 * half :])
        )

    cross = product(far)
    cut = m // 2
    via_in = send(cross[:cut].astype(bf16), in_run)
    via_out = send(cross[cut:m].astype(bf16), out_run)
    straight = product(near)
    to_out = cross[m:] + jnp.pad(via_in.astype(jnp.float32), ((0, m - cut), (0, 0)))
    to_in = straight[m:] + jnp.pad(via_out.astype(jnp.float32), ((cut, 0), (0, 0)))
    from_out = send(to_out.astype(bf16), out_run)
    from_in = send(to_in.astype(bf16), in_run)
    total = straight[:m] + from_out.astype(jnp.float32) + from_in.astype(jnp.float32)
    return total.astype(bf16)


def solution(mesh):
    fine = Mesh(mesh.devices.reshape(SIZES), AXES)
    row, col = ("y", "xl", "core"), ("z", "xh")
    return jax.shard_map(
        on_device,
        mesh=fine,
        in_specs=(P(row, col), P(None, row), P(row, col)),
        out_specs=P(row, col),
        check_vma=False,
    )
```

```python
import jax
import jax.numpy as jnp
from jax import lax
from jax.sharding import Mesh, PartitionSpec as P

AXES = ("y", "xl", "core", "z", "xh")
SIZES = (4, 2, 2, 8, 2)
ORDER = (0, 1, 7, 2, 6, 3, 5, 4)


def pairs(move):
    ids = {}
    for i in range(256):
        rest, at = i, []
        for size in reversed(SIZES):
            at.append(rest % size)
            rest //= size
        ids[tuple(reversed(at))] = i
    return [(i, ids[move(*at)]) for at, i in ids.items()]


def send(value, move):
    return lax.ppermute(value, AXES, pairs(move))


def other_core(y, xl, co, z, xh):
    return y, xl, 1 - co, z, xh


def z_by(step):
    return lambda y, xl, co, z, xh: (y, xl, co, (z + step) % 8, xh)


def y_by(step):
    return lambda y, xl, co, z, xh: ((y + step) % 4, xl, co, z, xh)


def rotated(stack, start):
    n = stack.shape[0]
    return lax.dynamic_slice_in_dim(jnp.concatenate([stack, stack]), start, n, 0)


def row_by(step, other):
    return lambda y, xl, co, z, xh: ((y + step) % 4, xl ^ other, co, z, xh)


def in_run(y, xl, co, z, xh):
    return y, 1 - xl, co, z, xh


def out_run(y, xl, co, z, xh):
    return y, 1 - xl, co, z, 1 - xh


def dot_f32(left, right):
    return lax.dot_general(
        left, right, (((1,), (1,)), ((), ())), preferred_element_type=jnp.float32
    )


def on_device(weight_tiles, expand_rows, expand_cols):
    y, xl, co, z, xh = (lax.axis_index(a) for a in AXES)
    bf16 = jnp.bfloat16
    k1, width = weight_tiles.shape
    half = width // 2
    m = expand_rows.shape[0] // 16
    n = expand_cols.shape[0]
    quarter = n // 4

    rows = expand_rows.reshape(4, 2, 2, m, k1)
    mine = lax.dynamic_index_in_dim(rows, co, 2, keepdims=False)
    theirs = lax.dynamic_index_in_dim(rows, 1 - co, 2, keepdims=False)
    got_rows = send(theirs, other_core)
    got_tiles = send(weight_tiles, other_core)

    pieces = [expand_cols[:, i * half : (i + 1) * half].reshape(4, 1, quarter, half) for i in range(2)]
    pieces = jnp.concatenate(pieces, 1).reshape(8, quarter, half)
    got_rows, got_tiles, pieces = lax.optimization_barrier((got_rows, got_tiles, pieces))
    pieces = lax.all_to_all(pieces, ("y", "xl"), 0, 0, tiled=True)

    left = jnp.concatenate([mine, got_rows], -1).reshape(8 * m, 2 * k1)
    right = jnp.concatenate([weight_tiles, got_tiles], 0)
    part = [
        jnp.dot(left, right[:, i * half : (i + 1) * half], preferred_element_type=jnp.float32)
        .astype(bf16).reshape(4, 2, m, half)
        for i in range(2)
    ]
    part = jnp.stack([part[0], part[1][:, ::-1]], 1).reshape(8, 2 * m, half)
    pieces = rotated(pieces, z)
    part, pieces = lax.optimization_barrier((part, pieces))
    barrier = lax.optimization_barrier
    part = lax.all_to_all(part, ("y", "xl"), 0, 0, tiled=True)

    got = {0: pieces[0]}
    for group in ((4, 3, 5, 1), (7, 2, 6)):
        got.update({i: send(pieces[-i % 8], z_by(-i)) for i in group})
        got, pieces = barrier((got, pieces))
    cols = jnp.concatenate([got[i] for i in ORDER], 1)
    part, cols = barrier((part, cols))
    inner = jnp.sum(part.astype(jnp.float32), 0).astype(bf16)

    up1, down1 = send(inner, z_by(-1)), send(inner, z_by(1))
    below, above = send(cols, y_by(1)), send(cols, y_by(-1))
    up2, down2 = send(up1, z_by(-1)), send(down1, z_by(1))
    first = jnp.concatenate((inner, up1, down1), 1)
    up2, down2, below, above, first = barrier((up2, down2, below, above, first))
    up3, down3 = send(up2, z_by(-1)), send(down2, z_by(1))
    far = [send(below[:, : 4 * half], y_by(1)), send(above[:, 4 * half :], y_by(-1))]
    second = jnp.concatenate((up2, down2), 1)
    up3, down3, far, second = barrier((up3, down3, far, second))
    full = jnp.zeros((n, 8 * half), bf16)
    for shift, block in ((0, cols), (1, above), (3, below), (2, jnp.concatenate(far, 1))):
        full = lax.dynamic_update_slice_in_dim(full, block, (y + shift) % 4 * quarter, 0)
    other = send(full, other_core)
    across = jnp.concatenate([send(up3[:m], z_by(-1)), send(down3[m:], z_by(1))])
    third = jnp.concatenate((up3, down3, across), 1)
    near = jnp.where(xh == co, full, other)
    far = jnp.where(xh == co, other, full)

    def product(side):
        return (
            dot_f32(first, side[:, : 3 * half])
            + dot_f32(second, side[:, 3 * half : 5 * half])
            + dot_f32(third, side[:, 5 * half :])
        )

    cross = product(far)
    cut = m // 2
    via_in = send(cross[:cut].astype(bf16), in_run)
    via_out = send(cross[cut:m].astype(bf16), out_run)
    straight = product(near)
    to_out = cross[m:] + jnp.pad(via_in.astype(jnp.float32), ((0, m - cut), (0, 0)))
    to_in = straight[m:] + jnp.pad(via_out.astype(jnp.float32), ((cut, 0), (0, 0)))
    from_out = send(to_out.astype(bf16), out_run)
    from_in = send(to_in.astype(bf16), in_run)
    total = straight[:m] + from_out.astype(jnp.float32) + from_in.astype(jnp.float32)
    return total.astype(bf16)


def solution(mesh):
    fine = Mesh(mesh.devices.reshape(SIZES), AXES)
    row, col = ("y", "xl", "core"), ("z", "xh")
    return jax.shard_map(
        on_device,
        mesh=fine,
        in_specs=(P(row, col), P(None, row), P(row, col)),
        out_specs=P(row, col),
        check_vma=False,
    )
```
